32 devices in a mesh: leaf: 16 (over z, y, x), dom: 2 (over core).
Axes of the slice: x: 2, y: 2, z: 4, core: 2. Of those that a mesh axis runs over, the one named last changes fastest.
Arguments:
- multipoles: float32 [2048, 64], P(('leaf', 'dom')), may hold values from -6 to 6
- positions: float32 [2048, 3, 256], P(('leaf', 'dom')), may hold values from 0 to 2
- charges: float32 [2048, 256], P(('leaf', 'dom')), may hold values from -6 to 6
- counts: int32 [2048], P(('leaf', 'dom')), may hold values from 1 to 256
- parents: float32 [256, 64], P('leaf', 'dom'), may hold values from -6 to 6
- parent_child_operators: float32 [8, 64, 64], replicated, may hold values from -0.75 to 0.75
- m2l: float32 [316, 64, 64], replicated, may hold values from -0.0625 to 0.0625
- m2l_list: int32 [2048, 316], P(('leaf', 'dom')), may hold values from -1 to 2047, as said below
- ulist: int32 [2048, 27], P(('leaf', 'dom')), may hold values from 0 to 2047, as said below
Outputs:
- locals_out: float32 [2048, 64], P(('leaf', 'dom'))
- near_field: float32 [2048, 256], P(('leaf', 'dom'))
The draws below stay inside these ranges and needn't reach their ends.
Inputs may be any that keep to these rules, and one draw needn't show every extreme that they name: `m2l_list`: every entry that is not -1 lies within 256 of its row's box index; in every row a box exactly 256 away is named in the first column. `ulist`: every entry lies within 256 of its row's box index; the first column names the row's own box, the second a box exactly 256 away.
All inputs are finite; a program needn't handle non-finite values.
Results may differ from the reference program's by a relative error of at most 0.0003.
Values sent between devices are 32-bit elements; how exact they have to be, the bound alone decides.
A program may use at most 64 MiB of HBM per device.

```python
import jax
import jax.numpy as jnp
from jax import lax

P_SIZE = 64
NV = 316
SMAX = 256
KU = 27
REACH = 4
BOX_DEV = 64
NB = 2048
NPAR = 256


def draw_m2l_list(key, part):
    key = jax.random.fold_in(key, 11)
    first, second = jax.random.split(key)
    reach = REACH * BOX_DEV
    rows = jnp.arange(NB, dtype=jnp.int32)[:, None]
    offset = jax.random.randint(first, (NB, NV), -reach, reach + 1)
    present = jax.random.randint(second, (NB, NV), 0, 5) < 3
    source = jnp.clip(rows + offset, 0, NB - 1)
    lists = jnp.where(present, source, -1)
    extreme = jnp.where(rows[:, 0] + reach < NB, rows[:, 0] + reach, rows[:, 0] - reach)
    return lists.at[:, 0].set(extreme).astype(jnp.int32)


def draw_ulist(key, part):
    key = jax.random.fold_in(key, 12)
    reach = REACH * BOX_DEV
    rows = jnp.arange(NB, dtype=jnp.int32)[:, None]
    offset = jax.random.randint(key, (NB, KU), -reach, reach + 1)
    lists = jnp.clip(rows + offset, 0, NB - 1)
    extreme = jnp.where(rows[:, 0] - reach >= 0, rows[:, 0] - reach, rows[:, 0] + reach)
    lists = lists.at[:, 0].set(rows[:, 0]).at[:, 1].set(extreme)
    return lists.astype(jnp.int32)


def draw_counts(key, part):
    key = jax.random.fold_in(key, 13)
    values = jax.random.randint(key, (NB,), 1, SMAX + 1)
    full = jnp.arange(NB, dtype=jnp.int32) % 8 == 3
    return jnp.where(full, SMAX, values).astype(jnp.int32)


def level_of(stream_key, dims, shards, smallest, largest):
    level, own = 1.0, jax.random.fold_in(stream_key, 6)
    for dim, shards_of in shards:
        heights = jnp.exp(jax.random.uniform(jax.random.fold_in(own, dim), (shards_of,), jnp.float32, smallest / len(shards), largest / len(shards)))
        level = level * jnp.repeat(heights, dims[dim] // shards_of).reshape([-1 if axis == dim else 1 for axis in range(len(dims))])
    return level


def normal_values(key, extent, spread, limit, cuts=(), held_as=jnp.bfloat16):
    factor_of = level_of(key, extent, cuts, -0.22, 0.18) if cuts else 1.0
    drawn = jax.random.normal(key, extent, jnp.float32) * spread * factor_of
    return jnp.minimum(jnp.maximum(drawn, -limit), limit).astype(held_as)


def setup_inputs(seed: int = 0) -> dict:
    key_of = jax.random.split(jax.random.key(seed), 10)
    return {
        "multipoles": normal_values(key_of[0], (NB, P_SIZE), 1.0, 6.0, ((0, 32),), jnp.float32),
        "positions": jnp.clip(2.0 * jax.random.uniform(key_of[1], (NB, 3, SMAX), jnp.float32) ** level_of(key_of[1], (NB, 3, SMAX), ((0, 32),), -0.2, 0.2), 0.0, 2.0),
        "charges": normal_values(key_of[2], (NB, SMAX), 1.0, 6.0, ((0, 32),), jnp.float32),
        "counts": draw_counts(jax.random.fold_in(key_of[9], 71), 0),
        "parents": normal_values(key_of[4], (NPAR, P_SIZE), 1.0, 6.0, ((0, 16), (1, 2)), jnp.float32),
        "parent_child_operators": normal_values(key_of[5], (8, P_SIZE, P_SIZE), P_SIZE ** -0.5, 0.75, (), jnp.float32),
        "m2l": normal_values(key_of[6], (NV, P_SIZE, P_SIZE), (P_SIZE * NV // 2) ** -0.5, 0.0625, (), jnp.float32),
        "m2l_list": draw_m2l_list(jax.random.fold_in(key_of[9], 71), 0),
        "ulist": draw_ulist(jax.random.fold_in(key_of[9], 71), 0),
    }


coef = 0.07957747154594767
soften = 0.0025

def near_block(targets, source_pos, source_chg):
    diff = targets[:, None, :, :, None] - source_pos[:, :, :, None, :]
    dist = lax.optimization_barrier(jnp.sum(diff * diff, axis=2))
    kernel = coef * lax.rsqrt(dist + soften)
    return jnp.einsum('bkts,bks->bt', kernel, source_chg, precision=lax.Precision.HIGHEST)

def reference(multipoles, positions, charges, counts, parents, parent_child_operators, m2l, m2l_list, ulist):
    leaf_box_list = positions.shape[0]
    slots = positions.shape[2]
    box_width = multipoles.shape[1]
    live = jnp.arange(slots, dtype=jnp.int32)[None, :] < counts[:, None]
    live_charge = jnp.where(live, charges, jnp.zeros_like(charges))
    child_octant = jnp.einsum('xky,dy->dxk', parent_child_operators, parents, precision=lax.Precision.HIGHEST).reshape(leaf_box_list, box_width)

    def far(lists):
        valid = lists >= 0
        picked = multipoles[jnp.clip(lists, 0, leaf_box_list - 1)] * valid[..., None].astype(multipoles.dtype)
        return jnp.einsum('bvq,vpq->bp', picked, m2l, precision=lax.Precision.HIGHEST)
    far_rows = lax.map(far, m2l_list.reshape(leaf_box_list // 64, 64, -1)).reshape(leaf_box_list, box_width)
    locals_out = child_octant + far_rows

    def near(args):
        targets, near_ids = args
        return near_block(targets, positions[near_ids], live_charge[near_ids])
    blocked = (positions.reshape(leaf_box_list // 2, 2, 3, slots), ulist.reshape(leaf_box_list // 2, 2, -1))
    near_field = lax.map(near, blocked).reshape(leaf_box_list, slots)
    return (locals_out, near_field)
```

```python
import functools

import jax
import jax.numpy as jnp
from jax import lax
from jax.experimental import pallas as pl
from jax.experimental.pallas import tpu as pltpu
from jax.sharding import PartitionSpec as P

REACH = 4
LANES = 128
CHUNK = 512


coef = 0.07957747154594767
soften = 0.0025


def split3(value):
    first = value.astype(jnp.bfloat16)
    rest = value - first.astype(jnp.float32)
    second = rest.astype(jnp.bfloat16)
    third = (rest - second.astype(jnp.float32)).astype(jnp.bfloat16)
    return first, second, third


def near_kernel(ku, slots, own_first, ids_ref, cnt_ref, feat_ref, out_ref, buf, tgt, acc):
    b = pl.program_id(0)
    blocks = slots // LANES
    per_chunk = CHUNK // LANES
    lane = lax.broadcasted_iota(jnp.int32, (8, LANES), 1)
    row = lax.broadcasted_iota(jnp.int32, (8, LANES), 0)
    blank = jnp.where(row == 4, 1.0, 0.0).astype(jnp.float32)

    own = feat_ref[own_first + b]
    wide_row = lax.broadcasted_iota(jnp.int32, (8, slots), 0)
    norm = jnp.broadcast_to(own[3:4, :], (8, slots)) + soften
    g = jnp.where(wide_row < 3, -2.0 * own, 0.0)
    g = jnp.where(wide_row == 3, 1.0, g)
    g = jnp.where(wide_row == 4, norm, g)
    g1, g2, g3 = (part.astype(jnp.float32) for part in split3(g))
    stacked = jnp.concatenate([g1, g1, g2, g2, g1, g3], axis=0)
    stacked = jnp.concatenate([stacked, jnp.zeros((LANES - 48, slots), jnp.float32)], axis=0)
    tgt[...] = stacked.T.astype(jnp.bfloat16)

    offset = jnp.int32(0)
    current = blank
    for k in range(ku):
        box = ids_ref[b * ku + k]
        live = cnt_ref[box]
        block = offset // LANES
        shift = offset % LANES
        keep = lane < shift
        rolled = [
            pltpu.roll(feat_ref[box, :, i * LANES : (i + 1) * LANES], shift, 1)
            for i in range(blocks)
        ]
        outs = [jnp.where(keep, current, rolled[0])]
        for i in range(1, blocks):
            outs.append(jnp.where(keep, rolled[i - 1], rolled[i]))
        outs.append(jnp.where(keep, rolled[-1], blank))
        for i, piece in enumerate(outs):
            buf[block + i] = piece
        offset = offset + live
        moved = offset // LANES - block
        current = outs[0]
        for i in range(1, blocks + 1):
            current = jnp.where(moved == i, outs[i], current)
    last = offset // LANES
    buf[last] = jnp.where(lane < offset % LANES, current, blank)
    for i in range(1, per_chunk):
        buf[last + i] = blank

    acc[...] = jnp.zeros_like(acc)

    def chunk_step(c, carry):
        feat = jnp.concatenate([buf[c * per_chunk + i] for i in range(per_chunk)], axis=1)
        f1, f2, f3 = (part.astype(jnp.float32) for part in split3(feat))
        source = jnp.concatenate(
            [f1, f2, f1, f2, f3, f1, jnp.zeros((LANES - 48, CHUNK), jnp.float32)], axis=0
        ).astype(jnp.bfloat16)
        dist = jnp.dot(tgt[...], source, preferred_element_type=jnp.float32)
        term = lax.rsqrt(dist) * feat[5:6, :]
        total = term[:, :LANES]
        for i in range(1, per_chunk):
            total = total + term[:, i * LANES : (i + 1) * LANES]
        acc[...] += total
        return carry

    chunks = (offset + CHUNK - 1) // CHUNK
    lax.fori_loop(0, chunks, chunk_step, 0)
    out_ref[0] = coef * jnp.sum(acc[...].T, axis=0, keepdims=True)


def near_call(ids, cnt, feat, boxes, own_first):
    slots = feat.shape[2]
    ku = ids.shape[0] // boxes
    room = (ku * slots + CHUNK) // LANES + slots // LANES + 2
    return pl.pallas_call(
        functools.partial(near_kernel, ku, slots, own_first),
        out_shape=jax.ShapeDtypeStruct((boxes, 1, slots), jnp.float32),
        grid_spec=pltpu.PrefetchScalarGridSpec(
            num_scalar_prefetch=2,
            grid=(boxes,),
            in_specs=[pl.BlockSpec(memory_space=pltpu.VMEM)],
            out_specs=pl.BlockSpec((1, 1, slots), lambda b, *_: (b, 0, 0)),
            scratch_shapes=[
                pltpu.VMEM((room, 8, LANES), jnp.float32),
                pltpu.VMEM((slots, LANES), jnp.bfloat16),
                pltpu.VMEM((slots, LANES), jnp.float32),
            ],
        ),
        compiler_params=pltpu.CompilerParams(vmem_limit_bytes=32 * 2**20),
    )(ids, cnt, feat)


def shifted(array, by):
    axis = ("leaf", "dom")
    devices = lax.axis_size(axis)
    pairs = [(i, i + by) for i in range(devices) if 0 <= i + by < devices]
    return lax.ppermute(array, axis, pairs)


def local(
    multipoles, positions, charges, counts, parents, parent_child_operators, m2l, m2l_list, ulist
):
    boxes = multipoles.shape[0]
    width = multipoles.shape[1]
    slots = charges.shape[1]
    groups = lax.axis_size("dom")
    half_id = lax.axis_index("dom")
    device = lax.axis_index("leaf") * groups + half_id
    live = jnp.arange(slots, dtype=jnp.int32)[None, :] < counts[:, None]
    live_charge = jnp.where(live, charges, jnp.zeros_like(charges))
    rest = jnp.concatenate(
        [
            multipoles,
            counts[:, None].astype(jnp.float32),
            jnp.zeros((boxes, slots - width - 1), jnp.float32),
        ],
        axis=1,
    )
    centred = jnp.transpose(positions, (1, 0, 2)) - 1.0
    packed = jnp.concatenate([centred, live_charge[None], rest[None]], axis=0)
    pieces = [packed if k == 0 else shifted(packed, -k) for k in range(-REACH, REACH + 1)]
    ext = jnp.concatenate(pieces, axis=1)

    family = boxes // 8
    whole = lax.all_gather(parents, "dom", axis=1, tiled=True)
    owned_boxes = lax.dynamic_slice_in_dim(whole, half_id * family, family, 0)
    child_octant = jnp.einsum(
        "xky,dy->dxk", parent_child_operators, owned_boxes, precision=lax.Precision.HIGHEST
    ).reshape(boxes, width)

    base = (device - REACH) * boxes
    extent = ext.shape[1]

    coords = ext[:3]
    norm = jnp.sum(coords * coords, axis=0)
    one = jnp.ones_like(norm)
    zero = jnp.zeros_like(norm)
    feat = jnp.stack([ext[0], ext[1], ext[2], norm, one, ext[3], zero, zero], axis=1)
    cnt = ext[4, :, width].astype(jnp.int32)
    near_ids = jnp.clip(ulist - base, 0, extent - 1).reshape(-1)
    near_field = near_call(near_ids, cnt, feat, boxes, REACH * boxes).reshape(boxes, slots)

    extended_multipoles = ext[4, :, :width]
    valid = m2l_list >= 0
    rows = jnp.clip(m2l_list - base, 0, extent - 1)
    picked = extended_multipoles[rows] * valid[..., None].astype(extended_multipoles.dtype)
    locals_out = child_octant + jnp.einsum(
        "bvq,vpq->bp", picked, m2l, precision=lax.Precision.HIGHEST
    )
    return (locals_out, near_field)


def solution(mesh):
    placed = (
        P(("leaf", "dom"), None),
        P(("leaf", "dom"), None, None),
        P(("leaf", "dom"), None),
        P(("leaf", "dom")),
        P("leaf", "dom"),
        P(),
        P(),
        P(("leaf", "dom"), None),
        P(("leaf", "dom"), None),
    )
    return jax.shard_map(
        local,
        mesh=mesh,
        in_specs=placed,
        out_specs=(P(("leaf", "dom"), None), P(("leaf", "dom"), None)),
        check_vma=False,
    )
```

```python
import functools

import jax
import jax.numpy as jnp
from jax import lax
from jax.experimental import pallas as pl
from jax.experimental.pallas import tpu as pltpu
from jax.sharding import PartitionSpec as P

REACH = 4
LANES = 128
WIDE = 8
MAIN = 4
TAIL = 8


coef = 0.07957747154594767
soften = 0.0025


def split3(value):
    first = value.astype(jnp.bfloat16)
    rest = value - first.astype(jnp.float32)
    second = rest.astype(jnp.bfloat16)
    third = (rest - second.astype(jnp.float32)).astype(jnp.bfloat16)
    return first, second, third


def near_kernel(
    ku, slots, boxes, own_first, ids_ref, cnt_ref, feat_ref, out_ref, even, odd, tgt, acc, lives
):
    pair = pl.program_id(0)
    blocks = slots // LANES
    lane = lax.broadcasted_iota(jnp.int32, (8, LANES), 1)
    row = lax.broadcasted_iota(jnp.int32, (8, LANES), 0)
    blank = jnp.where(row == 4, 1.0, 0.0).astype(jnp.float32)

    def collect(b, buf, slot):
        offset = jnp.int32(0)
        current = blank
        for k in range(ku):
            box = ids_ref[b * ku + k]
            live = cnt_ref[box]
            block = offset // LANES
            shift = offset % LANES
            keep = lane < shift
            rolled = [
                pltpu.roll(feat_ref[box, :, i * LANES : (i + 1) * LANES], shift, 1)
                for i in range(blocks)
            ]
            outs = [jnp.where(keep, current, rolled[0])]
            for i in range(1, blocks):
                outs.append(jnp.where(keep, rolled[i - 1], rolled[i]))
            outs.append(jnp.where(keep, rolled[-1], blank))
            for i, piece in enumerate(outs):
                buf[block + i] = piece
            offset = offset + live
            moved = offset // LANES - block
            current = outs[0]
            for i in range(1, blocks + 1):
                current = jnp.where(moved == i, outs[i], current)
        lives[slot] = offset

    def prepare(b):
        own = feat_ref[own_first + b]
        wide_row = lax.broadcasted_iota(jnp.int32, (8, slots), 0)
        norm = jnp.broadcast_to(own[3:4, :], (8, slots)) + soften
        g = jnp.where(wide_row < 3, -2.0 * own, 0.0)
        g = jnp.where(wide_row == 3, 1.0, g)
        g = jnp.where(wide_row == 4, norm, g)
        g1, g2, g3 = (part.astype(jnp.float32) for part in split3(g))
        stacked = jnp.concatenate([g1, g1, g2, g2, g1, g3], axis=0)
        stacked = jnp.concatenate([stacked, jnp.zeros((LANES - 48, slots), jnp.float32)], axis=0)
        tgt[...] = stacked.T.astype(jnp.bfloat16)

    def chunk_sum(buf, first, count, total_live):
        size = count * LANES
        feat = jnp.concatenate([buf[first + i] for i in range(count)], axis=1)
        f1, f2, f3 = (part.astype(jnp.float32) for part in split3(feat))
        source = jnp.concatenate(
            [f1, f2, f1, f2, f3, f1, jnp.zeros((LANES - 48, size), jnp.float32)], axis=0
        ).astype(jnp.bfloat16)
        dist = jnp.dot(tgt[...], source, preferred_element_type=jnp.float32)
        index = lax.broadcasted_iota(jnp.int32, (1, size), 1) + first * LANES
        charge = jnp.where(index < total_live, feat[5:6, :], 0.0)
        term = lax.rsqrt(dist) * charge
        total = term[:, :LANES]
        for i in range(1, count):
            total = total + term[:, i * LANES : (i + 1) * LANES]
        return total

    def target(slot, buf, fill, fill_slot, follower):
        live = lives[slot]
        prepare(2 * pair + slot)
        collect(follower, fill, fill_slot)
        total = chunk_sum(buf, 0, WIDE, live)
        for i in range(1, MAIN):
            total = total + chunk_sum(buf, i * WIDE, WIDE, live)
        acc[...] = total

        def rest(c, carry):
            acc[...] += chunk_sum(buf, MAIN * WIDE + c * TAIL, TAIL, live)
            return carry

        left = jnp.maximum(live - MAIN * WIDE * LANES, 0)
        lax.fori_loop(0, (left + TAIL * LANES - 1) // (TAIL * LANES), rest, 0)
        out_ref[slot] = coef * jnp.sum(acc[...].T, axis=0, keepdims=True)

    @pl.when(pair == 0)
    def _():
        def clear(i, carry):
            even[i] = blank
            odd[i] = blank
            return carry

        lax.fori_loop(0, even.shape[0], clear, 0)
        collect(0, even, 0)

    target(0, even, odd, 1, 2 * pair + 1)
    target(1, odd, even, 0, jnp.minimum(2 * pair + 2, boxes - 1))


def near_call(ids, cnt, feat, boxes, own_first):
    slots = feat.shape[2]
    ku = ids.shape[0] // boxes
    room = max(ku * slots // LANES, MAIN * WIDE) + TAIL + slots // LANES + 2
    return pl.pallas_call(
        functools.partial(near_kernel, ku, slots, boxes, own_first),
        out_shape=jax.ShapeDtypeStruct((boxes, 1, slots), jnp.float32),
        grid_spec=pltpu.PrefetchScalarGridSpec(
            num_scalar_prefetch=2,
            grid=(boxes // 2,),
            in_specs=[pl.BlockSpec(memory_space=pltpu.VMEM)],
            out_specs=pl.BlockSpec((2, 1, slots), lambda b, *_: (b, 0, 0)),
            scratch_shapes=[
                pltpu.VMEM((room, 8, LANES), jnp.float32),
                pltpu.VMEM((room, 8, LANES), jnp.float32),
                pltpu.VMEM((slots, LANES), jnp.bfloat16),
                pltpu.VMEM((slots, LANES), jnp.float32),
                pltpu.SMEM((2,), jnp.int32),
            ],
        ),
        compiler_params=pltpu.CompilerParams(vmem_limit_bytes=40 * 2**20),
    )(ids, cnt, feat)


def far_kernel(width, per, blocks, mult_ref, list_ref, ops_ref, out_ref, table, acc):
    extent = mult_ref.shape[1]
    cols = list_ref.shape[2]
    mult = mult_ref[...]
    high = mult.astype(jnp.bfloat16)
    low = (mult - high.astype(jnp.float32)).astype(jnp.bfloat16)
    for i, part in enumerate((high, low, high, low)):
        table[i * width : (i + 1) * width, :] = part
    acc[...] = jnp.zeros_like(acc)
    source = lax.broadcasted_iota(jnp.int32, (extent, cols), 0)

    def product(step):
        chosen = (source == list_ref[step]).astype(jnp.float32).astype(jnp.bfloat16)
        picked = jnp.dot(table[...], chosen, preferred_element_type=jnp.float32)
        op = ops_ref[step]
        op = jnp.concatenate([op, op], axis=1)
        op_high = op.astype(jnp.bfloat16)
        op_low = (op - op_high.astype(jnp.float32)).astype(jnp.bfloat16)
        weights = jnp.concatenate([op_high, op_low], axis=1)
        return jnp.dot(weights, picked.astype(jnp.bfloat16), preferred_element_type=jnp.float32)

    group = 3

    def group_step(i, carry):
        total = product(i * group)
        for j in range(1, group):
            total = total + product(i * group + j)
        acc[...] += total
        return carry

    lax.fori_loop(0, blocks // group, group_step, 0)
    for step in range(blocks // group * group, blocks):
        acc[...] += product(step)
    boxes = cols // per
    total = acc[:width, :boxes]
    for i in range(1, per):
        total = total + acc[i * width : (i + 1) * width, i * boxes : (i + 1) * boxes]
    out_ref[...] = total.T


def far_call(mult, lists, m2l, boxes):
    vectors, width = m2l.shape[0], m2l.shape[1]
    per = 4
    blocks = vectors // per
    extent = -(-mult.shape[1] // LANES) * LANES
    mult = jnp.pad(mult, ((0, 0), (0, extent - mult.shape[1])))
    lists = lists.T.reshape(blocks, 1, per * boxes)
    ops = m2l.reshape(blocks, per * width, width)
    return pl.pallas_call(
        functools.partial(far_kernel, width, per, blocks),
        out_shape=jax.ShapeDtypeStruct((boxes, width), jnp.float32),
        in_specs=[pl.BlockSpec(memory_space=pltpu.VMEM)] * 3,
        out_specs=pl.BlockSpec(memory_space=pltpu.VMEM),
        scratch_shapes=[
            pltpu.VMEM((4 * width, extent), jnp.bfloat16),
            pltpu.VMEM((per * width, per * boxes), jnp.float32),
        ],
        cost_estimate=pl.CostEstimate(
            flops=60_000_000_000, bytes_accessed=12_000_000, transcendentals=0
        ),
        compiler_params=pltpu.CompilerParams(vmem_limit_bytes=32 * 2**20),
    )(mult, lists, ops)


def shifted(array, by):
    axis = ("leaf", "dom")
    devices = lax.axis_size(axis)
    pairs = [(i, i + by) for i in range(devices) if 0 <= i + by < devices]
    return lax.ppermute(array, axis, pairs)


def halo(array):
    return [array if k == 0 else shifted(array, -k) for k in range(-REACH, REACH + 1)]


def local(
    multipoles, positions, charges, counts, parents, parent_child_operators, m2l, m2l_list, ulist
):
    boxes = multipoles.shape[0]
    width = multipoles.shape[1]
    slots = charges.shape[1]
    groups = lax.axis_size("dom")
    half_id = lax.axis_index("dom")
    device = lax.axis_index("leaf") * groups + half_id
    live = jnp.arange(slots, dtype=jnp.int32)[None, :] < counts[:, None]
    live_charge = jnp.where(live, charges, jnp.zeros_like(charges))
    centred = jnp.transpose(positions, (1, 0, 2)) - 1.0
    packed = jnp.concatenate([centred, live_charge[None]], axis=0)
    rest = jnp.concatenate(
        [
            multipoles.T,
            jnp.broadcast_to(counts.astype(jnp.float32)[None, :], (8, boxes)),
        ],
        axis=0,
    )
    ext_rest = jnp.concatenate(halo(rest), axis=1)
    ext = jnp.concatenate(halo(packed), axis=1)

    family = boxes // 8
    whole = lax.all_gather(parents, "dom", axis=1, tiled=True)
    owned_boxes = lax.dynamic_slice_in_dim(whole, half_id * family, family, 0)
    child_octant = jnp.einsum(
        "xky,dy->dxk", parent_child_operators, owned_boxes, precision=lax.Precision.HIGHEST
    ).reshape(boxes, width)

    base = (device - REACH) * boxes
    extent = ext.shape[1]

    coords = ext[:3]
    norm = jnp.sum(coords * coords, axis=0)
    one = jnp.ones_like(norm)
    zero = jnp.zeros_like(norm)
    feat = jnp.stack([ext[0], ext[1], ext[2], norm, one, ext[3], zero, zero], axis=1)
    cnt = ext_rest[width].astype(jnp.int32)
    near_ids = jnp.clip(ulist - base, 0, extent - 1).reshape(-1)
    near_field = near_call(near_ids, cnt, feat, boxes, REACH * boxes).reshape(boxes, slots)

    rows = jnp.where(m2l_list >= 0, jnp.clip(m2l_list - base, 0, extent - 1), -1)
    locals_out = child_octant + far_call(ext_rest[:width], rows, m2l, boxes)
    return (locals_out, near_field)


def solution(mesh):
    placed = (
        P(("leaf", "dom"), None),
        P(("leaf", "dom"), None, None),
        P(("leaf", "dom"), None),
        P(("leaf", "dom")),
        P("leaf", "dom"),
        P(),
        P(),
        P(("leaf", "dom"), None),
        P(("leaf", "dom"), None),
    )
    return jax.shard_map(
        local,
        mesh=mesh,
        in_specs=placed,
        out_specs=(P(("leaf", "dom"), None), P(("leaf", "dom"), None)),
        check_vma=False,
    )
```

```python
import functools

import jax
import jax.numpy as jnp
from jax import lax
from jax.experimental import pallas as pl
from jax.experimental.pallas import tpu as pltpu
from jax.sharding import PartitionSpec as P

REACH = 4
LANES = 128
WIDE = 8
MAIN = 4
TAIL = 8


coef = 0.07957747154594767
soften = 0.0025


def split3(value):
    first = value.astype(jnp.bfloat16)
    rest = value - first.astype(jnp.float32)
    second = rest.astype(jnp.bfloat16)
    third = (rest - second.astype(jnp.float32)).astype(jnp.bfloat16)
    return first, second, third


def near_kernel(
    ku, slots, boxes, own_first, ids_ref, cnt_ref, ext_ref, out_ref, feat_ref, even, odd, tgt, acc, lives
):
    pair = pl.program_id(0)
    blocks = slots // LANES
    lane = lax.broadcasted_iota(jnp.int32, (8, LANES), 1)
    row = lax.broadcasted_iota(jnp.int32, (8, LANES), 0)
    blank = jnp.where(row == 4, 1.0, 0.0).astype(jnp.float32)

    def collect(b, buf, slot):
        offset = jnp.int32(0)
        current = blank
        for k in range(ku):
            box = ids_ref[b * ku + k]
            live = cnt_ref[box]
            block = offset // LANES
            shift = offset % LANES
            keep = lane < shift
            rolled = [
                pltpu.roll(feat_ref[box, :, i * LANES : (i + 1) * LANES], shift, 1)
                for i in range(blocks)
            ]
            outs = [jnp.where(keep, current, rolled[0])]
            for i in range(1, blocks):
                outs.append(jnp.where(keep, rolled[i - 1], rolled[i]))
            outs.append(jnp.where(keep, rolled[-1], blank))
            for i, piece in enumerate(outs):
                buf[block + i] = piece
            offset = offset + live
            moved = offset // LANES - block
            current = outs[0]
            for i in range(1, blocks + 1):
                current = jnp.where(moved == i, outs[i], current)
        lives[slot] = offset

    def prepare(b):
        own = feat_ref[own_first + b]
        wide_row = lax.broadcasted_iota(jnp.int32, (8, slots), 0)
        norm = jnp.broadcast_to(own[3:4, :], (8, slots)) + soften
        g = jnp.where(wide_row < 3, -2.0 * own, 0.0)
        g = jnp.where(wide_row == 3, 1.0, g)
        g = jnp.where(wide_row == 4, norm, g)
        g1, g2, g3 = (part.astype(jnp.float32) for part in split3(g))
        stacked = jnp.concatenate([g1, g1, g2, g2, g1, g3], axis=0)
        stacked = jnp.concatenate([stacked, jnp.zeros((LANES - 48, slots), jnp.float32)], axis=0)
        tgt[...] = stacked.T.astype(jnp.bfloat16)

    def chunk_sum(buf, first, count, total_live):
        size = count * LANES
        feat = jnp.concatenate([buf[first + i] for i in range(count)], axis=1)
        f1, f2, f3 = (part.astype(jnp.float32) for part in split3(feat))
        source = jnp.concatenate(
            [f1, f2, f1, f2, f3, f1, jnp.zeros((LANES - 48, size), jnp.float32)], axis=0
        ).astype(jnp.bfloat16)
        dist = jnp.dot(tgt[...], source, preferred_element_type=jnp.float32)
        index = lax.broadcasted_iota(jnp.int32, (1, size), 1) + first * LANES
        charge = jnp.where(index < total_live, feat[5:6, :], 0.0)
        term = lax.rsqrt(dist) * charge
        total = term[:, :LANES]
        for i in range(1, count):
            total = total + term[:, i * LANES : (i + 1) * LANES]
        return total

    def target(slot, buf, fill, fill_slot, follower):
        live = lives[slot]
        prepare(2 * pair + slot)
        collect(follower, fill, fill_slot)
        total = chunk_sum(buf, 0, WIDE, live)
        for i in range(1, MAIN):
            total = total + chunk_sum(buf, i * WIDE, WIDE, live)
        acc[...] = total

        def rest(c, carry):
            acc[...] += chunk_sum(buf, MAIN * WIDE + c * TAIL, TAIL, live)
            return carry

        left = jnp.maximum(live - MAIN * WIDE * LANES, 0)
        lax.fori_loop(0, (left + TAIL * LANES - 1) // (TAIL * LANES), rest, 0)
        out_ref[slot] = coef * jnp.sum(acc[...].T, axis=0, keepdims=True)

    @pl.when(pair == 0)
    def _():
        def clear(i, carry):
            even[i] = blank
            odd[i] = blank
            return carry

        lax.fori_loop(0, even.shape[0], clear, 0)

        tall = lax.broadcasted_iota(jnp.int32, (8, slots), 0)

        def features(i, carry):
            first = pl.multiple_of(i * 8, 8)
            x, y, z, charge = (ext_ref[r, pl.ds(first, 8), :] for r in range(4))
            norm = x * x + y * y + z * z
            for j in range(8):
                made = jnp.where(tall == 4, 1.0, 0.0)
                for r, part in ((0, x), (1, y), (2, z), (3, norm), (5, charge)):
                    line = jnp.broadcast_to(part[j : j + 1, :], (8, slots))
                    made = jnp.where(tall == r, line, made)
                feat_ref[first + j] = made
            return carry

        lax.fori_loop(0, feat_ref.shape[0] // 8, features, 0)
        collect(0, even, 0)

    target(0, even, odd, 1, 2 * pair + 1)
    target(1, odd, even, 0, jnp.minimum(2 * pair + 2, boxes - 1))


def near_call(ids, cnt, ext, boxes, own_first):
    slots = ext.shape[2]
    ku = ids.shape[0] // boxes
    room = max(ku * slots // LANES, MAIN * WIDE) + TAIL + slots // LANES + 2
    return pl.pallas_call(
        functools.partial(near_kernel, ku, slots, boxes, own_first),
        out_shape=jax.ShapeDtypeStruct((boxes, 1, slots), jnp.float32),
        grid_spec=pltpu.PrefetchScalarGridSpec(
            num_scalar_prefetch=2,
            grid=(boxes // 2,),
            in_specs=[pl.BlockSpec(memory_space=pltpu.VMEM)],
            out_specs=pl.BlockSpec((2, 1, slots), lambda b, *_: (b, 0, 0)),
            scratch_shapes=[
                pltpu.VMEM((ext.shape[1], 8, slots), jnp.float32),
                pltpu.VMEM((room, 8, LANES), jnp.float32),
                pltpu.VMEM((room, 8, LANES), jnp.float32),
                pltpu.VMEM((slots, LANES), jnp.bfloat16),
                pltpu.VMEM((slots, LANES), jnp.float32),
                pltpu.SMEM((2,), jnp.int32),
            ],
        ),
        compiler_params=pltpu.CompilerParams(vmem_limit_bytes=40 * 2**20),
    )(ids, cnt, ext)


def far_kernel(width, per, blocks, mult_ref, list_ref, ops_ref, out_ref, table, acc):
    extent = mult_ref.shape[1]
    cols = list_ref.shape[2]
    mult = mult_ref[...]
    high = mult.astype(jnp.bfloat16)
    low = (mult - high.astype(jnp.float32)).astype(jnp.bfloat16)
    for i, part in enumerate((high, low, high, low)):
        table[i * width : (i + 1) * width, :] = part
    acc[...] = jnp.zeros_like(acc)
    source = lax.broadcasted_iota(jnp.int32, (extent, cols), 0)

    def product(step):
        chosen = (source == list_ref[step]).astype(jnp.float32).astype(jnp.bfloat16)
        picked = jnp.dot(table[...], chosen, preferred_element_type=jnp.float32)
        op = ops_ref[pl.ds(step * per, per)].reshape(per * width, width)
        op = jnp.concatenate([op, op], axis=1)
        op_high = op.astype(jnp.bfloat16)
        op_low = (op - op_high.astype(jnp.float32)).astype(jnp.bfloat16)
        weights = jnp.concatenate([op_high, op_low], axis=1)
        return jnp.dot(weights, picked.astype(jnp.bfloat16), preferred_element_type=jnp.float32)

    group = 3

    def group_step(i, carry):
        total = product(i * group)
        for j in range(1, group):
            total = total + product(i * group + j)
        acc[...] += total
        return carry

    lax.fori_loop(0, blocks // group, group_step, 0)
    for step in range(blocks // group * group, blocks):
        acc[...] += product(step)
    boxes = cols // per
    total = acc[:width, :boxes]
    for i in range(1, per):
        total = total + acc[i * width : (i + 1) * width, i * boxes : (i + 1) * boxes]
    out_ref[...] = total.T


def far_call(mult, lists, m2l, boxes):
    vectors, width = m2l.shape[0], m2l.shape[1]
    per = 4
    blocks = vectors // per
    extent = -(-mult.shape[1] // LANES) * LANES
    mult = jnp.pad(mult, ((0, 0), (0, extent - mult.shape[1])))
    lists = lists.T.reshape(blocks, 1, per * boxes)
    return pl.pallas_call(
        functools.partial(far_kernel, width, per, blocks),
        out_shape=jax.ShapeDtypeStruct((boxes, width), jnp.float32),
        in_specs=[pl.BlockSpec(memory_space=pltpu.VMEM)] * 3,
        out_specs=pl.BlockSpec(memory_space=pltpu.VMEM),
        scratch_shapes=[
            pltpu.VMEM((4 * width, extent), jnp.bfloat16),
            pltpu.VMEM((per * width, per * boxes), jnp.float32),
        ],
        cost_estimate=pl.CostEstimate(
            flops=60_000_000_000, bytes_accessed=12_000_000, transcendentals=0
        ),
        compiler_params=pltpu.CompilerParams(vmem_limit_bytes=32 * 2**20),
    )(mult, lists, m2l)


def shifted(array, by):
    axis = ("leaf", "dom")
    devices = lax.axis_size(axis)
    pairs = [(i, i + by) for i in range(devices) if 0 <= i + by < devices]
    return lax.ppermute(array, axis, pairs)


def halo(array):
    return [array if k == 0 else shifted(array, -k) for k in range(-REACH, REACH + 1)]


def local(
    multipoles, positions, charges, counts, parents, parent_child_operators, m2l, m2l_list, ulist
):
    boxes = multipoles.shape[0]
    width = multipoles.shape[1]
    slots = charges.shape[1]
    groups = lax.axis_size("dom")
    half_id = lax.axis_index("dom")
    device = lax.axis_index("leaf") * groups + half_id
    live = jnp.arange(slots, dtype=jnp.int32)[None, :] < counts[:, None]
    live_charge = jnp.where(live, charges, jnp.zeros_like(charges))
    centred = jnp.transpose(positions, (1, 0, 2)) - 1.0
    packed = jnp.concatenate([centred, live_charge[None]], axis=0)
    rest = jnp.concatenate(
        [
            multipoles.T,
            jnp.broadcast_to(counts.astype(jnp.float32)[None, :], (8, boxes)),
        ],
        axis=0,
    )
    ext_rest = jnp.concatenate(halo(rest), axis=1)
    ext = jnp.concatenate(halo(packed), axis=1)

    family = boxes // 8
    whole = lax.all_gather(parents, "dom", axis=1, tiled=True)
    owned_boxes = lax.dynamic_slice_in_dim(whole, half_id * family, family, 0)
    child_octant = jnp.einsum(
        "xky,dy->dxk", parent_child_operators, owned_boxes, precision=lax.Precision.HIGHEST
    ).reshape(boxes, width)

    base = (device - REACH) * boxes
    extent = ext.shape[1]

    cnt = ext_rest[width].astype(jnp.int32)
    near_ids = jnp.clip(ulist - base, 0, extent - 1).reshape(-1)
    near_field = near_call(near_ids, cnt, ext, boxes, REACH * boxes).reshape(boxes, slots)

    rows = jnp.where(m2l_list >= 0, jnp.clip(m2l_list - base, 0, extent - 1), -1)
    locals_out = child_octant + far_call(ext_rest[:width], rows, m2l, boxes)
    return (locals_out, near_field)


def solution(mesh):
    placed = (
        P(("leaf", "dom"), None),
        P(("leaf", "dom"), None, None),
        P(("leaf", "dom"), None),
        P(("leaf", "dom")),
        P("leaf", "dom"),
        P(),
        P(),
        P(("leaf", "dom"), None),
        P(("leaf", "dom"), None),
    )
    return jax.shard_map(
        local,
        mesh=mesh,
        in_specs=placed,
        out_specs=(P(("leaf", "dom"), None), P(("leaf", "dom"), None)),
        check_vma=False,
    )
```
